256 devices in a mesh: row: 8 (over y, core), col: 32 (over x, z).
Axes of the slice: x: 4, y: 4, z: 8, core: 2. Of those that a mesh axis runs over, the one named last changes fastest.
Arguments:
- span: bfloat16 [1024, 16384], P('col', 'row'), may hold values from -6 to 6
- gram: float32 [16384, 16384], P('row', 'col'), may hold values from -0.08 to 0.08
- ridge: float32 [16384], P('row'), may hold values from 4 to 8
Outputs:
- factored: float32 [16384, 16384], P('row', 'col')
The draws below stay inside these ranges and needn't reach their ends.
All inputs are finite; a program needn't handle non-finite values.
Results may differ from the reference program's by a relative error of at most 0.005.
Values may be sent and summed in bfloat16 or wider, within the bound.
A program may use at most 64 MiB of HBM per device.

```python
import math
import jax
import jax.numpy as jnp
from jax import lax

G = 16384
NB = 512
TOKENS = 1024
N_ROW = 8
N_COL = 32


def block_scale(rng, extent, cuts, least, high):
    gain = 1.0
    for axis_at, shards_of in cuts:
        draws = jax.random.uniform(jax.random.fold_in(jax.random.fold_in(rng, 6), axis_at), (shards_of,), jnp.float32, least / len(cuts), high / len(cuts))
        gain = gain * jnp.repeat(jnp.exp(draws), extent[axis_at] // shards_of).reshape((-1,) + (1,) * (len(extent) - 1 - axis_at))
    return gain


def bell_draw(stream_key, extent, deviation, reach, split=(), kind=jnp.bfloat16):
    level = block_scale(stream_key, extent, split, -0.22, 0.18) if split else 1.0
    drawn = jax.random.normal(stream_key, extent, jnp.float32) * deviation * level
    return jnp.minimum(jnp.maximum(drawn, -reach), reach).astype(kind)


def setup_inputs(seed: int = 0) -> dict:
    key_of = jax.random.split(jax.random.key(seed), 4)
    span = bell_draw(key_of[0], (TOKENS, G), 1.0, 6.0, ((0, 32), (1, 8)))
    gram = jnp.clip(jax.random.uniform(key_of[1], (G, G), jnp.float32, -0.08, 0.08) * block_scale(key_of[1], (G, G), ((0, 8), (1, 32)), -0.4, 0.0), -0.08, 0.08)
    ridge = jnp.clip(jnp.exp(math.log(8.0) - 0.6931472 * jax.random.uniform(key_of[2], (G,), jnp.float32) ** block_scale(key_of[2], (G,), ((0, 8),), -0.2, 0.2)), 4.0, 8.0)
    return {"span": span, "gram": gram, "ridge": ridge}


def to_logical(matrix, axis, groups):
    shape = matrix.shape
    within = shape[axis] // (groups * NB)
    reshaped = matrix.reshape(shape[:axis] + (groups, within, NB) + shape[axis + 1:])
    return jnp.swapaxes(reshaped, axis, axis + 1).reshape(shape)

def to_stored(matrix, axis, groups):
    shape = matrix.shape
    within = shape[axis] // (groups * NB)
    reshaped = matrix.reshape(shape[:axis] + (within, groups, NB) + shape[axis + 1:])
    return jnp.swapaxes(reshaped, axis, axis + 1).reshape(shape)

def reference(span, gram, ridge):
    features = to_logical(span, 1, N_ROW)
    accum = to_logical(to_logical(gram, 0, N_ROW), 1, N_COL)
    accum = accum + jnp.dot(features.T.astype(jnp.float32), features.astype(jnp.float32), preferred_element_type=jnp.float32) / TOKENS
    diag_index = jnp.arange(G)
    accum = accum.at[diag_index, diag_index].add(to_logical(ridge, 0, N_ROW))
    corner = accum[:NB, :NB]
    symmetric = jnp.tril(corner) + jnp.tril(corner, -1).T
    lower_part = jnp.linalg.cholesky(symmetric)
    panel_rows = jax.scipy.linalg.solve_triangular(lower_part, accum[NB:, :NB].T, lower=True).T
    trailing = accum[NB:, NB:] - jnp.dot(panel_rows, panel_rows.T, precision=lax.Precision.HIGHEST)
    upper_band = jnp.concatenate([lower_part, accum[:NB, NB:]], axis=1)
    lower_band = jnp.concatenate([panel_rows, trailing], axis=1)
    result = jnp.concatenate([upper_band, lower_band], axis=0)
    return to_stored(to_stored(result, 0, N_ROW), 1, N_COL)
```

```python
import jax
import jax.numpy as jnp
from jax import lax
from jax.experimental import pallas as pl
from jax.experimental.pallas import tpu as pltpu
from jax.sharding import PartitionSpec as P

NB = 512
NX, NZ, NROW = 4, 8, 8
NCOL = NX * NZ
TOKENS = 1024
ORDER = (0, -1, 1, -2, 2, -3, 3, 4)
MESH = pl.DeviceIdType.MESH
HI = lax.Precision.HIGHEST
F32, BF16 = jnp.float32, jnp.bfloat16
TN = (((0,), (0,)), ((), ()))


def eye(n):
    return (lax.broadcasted_iota(jnp.int32, (n, n), 0)
            == lax.broadcasted_iota(jnp.int32, (n, n), 1)).astype(F32)


def factor_block(d, between):
    n = d.shape[0]
    rows = lax.broadcasted_iota(jnp.int32, (8, n), 0)
    e = eye(n)
    done = []
    for p in range(n // 8):
        left = n - 8 * p
        if p % 4 == 0:
            between(p // 4)
        cols = [jnp.broadcast_to(d[:, 8 * p + j:8 * p + j + 1], (left, n)) for j in range(8)]
        pivots = jnp.ones((8, n), F32)
        for j in range(8):
            pivot = cols[j][j:j + 1]
            pivots = jnp.where(rows == j, pivot, pivots)
            f = cols[j] * (1.0 / pivot)
            head = jnp.where(rows > j, f[:8], 0.0)
            f = jnp.concatenate([head, f[8:]], axis=0) if left > 8 else head
            d = d - f * d[j:j + 1]
            e = e - f * e[j:j + 1]
            for k in range(j + 1, 8):
                cols[k] = cols[k] - f * cols[k][j:j + 1]
        done.append(e[:8] * lax.rsqrt(pivots))
        if left > 8:
            d, e = d[8:], e[8:]
    return jnp.concatenate(done, axis=0)


def split(a):
    high = a.astype(BF16)
    return high, (a - high.astype(F32)).astype(BF16)


def panel_kernel(span, gram, ridge, acc_out, a0_out, z_out,
                 sg, g0, ea, sc, gc, yg, rr, piece, gv, gb, w, p0, acc, a0, zv,
                 q, ssem, rsem, lsem, pcs, pcr):
    r = lax.axis_index("row")
    c = lax.axis_index("col")
    x, z = c // NZ, c % NZ
    core = r % 2
    other = r + 1 - 2 * core
    zp, zm = x * NZ + (z + 1) % NZ, x * NZ + (z + NZ - 1) % NZ
    xp, xm = (x + 1) % NX * NZ + z, (x + NX - 1) % NX * NZ + z
    xs = {d: (x + NX + d) % NX for d in (-1, 0, 1, 2)}
    zs = {d: (z + NZ + d) % NZ for d in range(-4, 5)}
    receiver = core == z % 2

    number, local_number = {}, {}
    phase = ["go"]

    def index(name):
        return number.setdefault(name, len(number))

    def remote(send_name, name, src, dst, dev):
        return pltpu.make_async_remote_copy(
            src_ref=src, dst_ref=dst, send_sem=ssem.at[index(send_name)], recv_sem=rsem.at[index(name)],
            device_id=dev, device_id_type=MESH)

    def local(name, src, dst):
        i = local_number.setdefault(name, len(local_number))
        return pltpu.make_async_copy(src, dst, lsem.at[i])

    def send(name, src, dst, dev):
        cp = remote(name, name, src, dst, dev)
        if phase[0] == "go":
            cp.start()
        else:
            cp.wait_send()

    def arrive(name, dst):
        if phase[0] == "go":
            remote(name, name, dst, dst, (r, zp)).wait_recv()

    barrier = pltpu.get_barrier_semaphore()
    for d in range(1, NROW):
        pl.semaphore_signal(barrier, inc=1, device_id=((r + d) % NROW, c), device_id_type=MESH)

    @pl.loop(1, NCOL)
    def _(t):
        pl.semaphore_signal(barrier, inc=1, device_id=(r, (c + t) % NCOL), device_id_type=MESH)

    lead, rest = pl.ds(0, NB), pl.ds(NB, 3 * NB)
    lead_in = local("lead", gram.at[lead], gv.at[lead])
    gram_in = local("gram", gram.at[rest], gv.at[rest])
    lead_in.start()
    gram_in.start()
    own = local("own", span, sg.at[x, z])
    own.start()

    def cast_panel(lo, hi):
        @pl.loop(lo, hi)
        def _(t):
            part = pl.ds(pl.multiple_of(t * 256, 256), 256)
            gb[part, :] = gv[part, :].astype(BF16)

    @pl.when(c == 0)
    def _():
        lead_in.wait()
        cast_panel(0, 2)
        gram_in.wait()
        cast_panel(2, 8)

    pl.semaphore_wait(barrier, NROW - 1 + NCOL - 1)

    tile0 = pl.ds(0, NB)

    def corner_piece(t):
        return pltpu.make_async_remote_copy(
            src_ref=gb.at[pl.ds(pl.multiple_of(t * 16, 16), 16)], dst_ref=piece,
            send_sem=pcs.at[t], recv_sem=pcr.at[0], device_id=(r, t), device_id_type=MESH)

    @pl.when(jnp.logical_and(r == 0, c == 0))
    def _():
        @pl.loop(1, NCOL)
        def _(t):
            corner_piece(t).start()

    def row0_copies(kind):
        cps = []
        for d in range(1, NROW):
            half = d % 2
            if kind == "g":
                cps.append(remote("g%d" % d, "eg", piece.at[:, pl.ds(half * 256, 256)],
                                  ea.at[x, z, half, :, pl.ds(NB, 256)], (d, c)))
            else:
                cps.append(remote("s%d" % d, "es", span.at[pl.ds(half * 16, 16), tile0],
                                  ea.at[x, z, half, :, pl.ds(0, NB)], (d, c)))
                cps.append(remote("r%d" % d, "er", ridge.at[pl.ds(0, 8)], rr, (d, c)))
        return cps

    own_s = local("own_s", span.at[pl.ds(0, 16), tile0], ea.at[x, z, 0, :, pl.ds(0, NB)])
    own_g = local("own_g", piece.at[:, pl.ds(0, 256)], ea.at[x, z, 0, :, pl.ds(NB, 256)])
    own_r = local("own_r", ridge.at[pl.ds(0, 8)], rr)

    @pl.when(r == 0)
    def _():
        for cp in row0_copies("s"):
            cp.start()
        own_s.start()
        own_r.start()

    def own_sends():
        send("zp0", span, sg.at[x, z], (r, zp))
        send("zm0", span, sg.at[x, z], (r, zm))
        send("xp0", span, sg.at[x, z], (r, xp))
        send("xm0", span, sg.at[x, z], (r, xm))

    g0_own = local("g0_own", gb.at[pl.ds(0, 64)], g0.at[0, 0])

    hubs = ((NZ, NZ), (3 * NZ, 3 * NZ), (1, 2 * NZ + 1), (NZ - 1, 2 * NZ + 5))

    def hub_copies():
        cps = []
        for hub, first in hubs:
            for h in range(2 if hub % NZ == 0 else 1):
                cps.append(remote("q%d%d" % (hub, h), "q%d" % h, gb.at[pl.ds((first + 4 * h) * 64, 256)],
                                  q.at[pl.ds(4 * h * 64, 256)], (r, hub)))
        cps[-1] = remote("q%d0" % (NZ - 1), "q0", gb.at[pl.ds((2 * NZ + 5) * 64, 192)],
                         q.at[pl.ds(0, 192)], (r, NZ - 1))
        cps.append(remote("q%d1" % (NZ - 1), "q1", gb.at[pl.ds(2 * NZ * 64, 64)],
                          q.at[pl.ds(192, 64)], (r, NZ - 1)))
        for t in range(1, NZ):
            cps.append(remote("p%d" % t, "piece", gb.at[pl.ds(t * 64, 64)], g0.at[0, t], (r, t)))
        return cps

    def hub_pass(h):
        for hub, first in hubs:
            if hub == 1:
                if h:
                    continue
                moves = [(i, 2, 1 + i) for i in range(4)]
            elif hub == NZ - 1:
                moves = [(i, 2, 5 + i) for i in range(3)] if h == 0 else [(3, 2, 0)]
            else:
                moves = [(i, hub // NZ, i) for i in range(4 * h, 4 * h + 4)]

            @pl.when(c == hub)
            def _():
                arrive("q%d" % h, q.at[pl.ds(moves[0][0] * 64, 64 * len(moves))])
                for i, xx, zz in moves:
                    src, dst = q.at[pl.ds(i * 64, 64)], g0.at[xx, zz]
                    if xx * NZ + zz == hub:
                        if phase[0] == "go":
                            local("g0_hub", src, dst).start()
                        continue
                    cp = remote("f%d" % i, "piece", src, dst, (r, xx * NZ + zz))
                    if phase[0] == "go":
                        cp.start()
                    else:
                        cp.wait_send()

    own_sends()

    @pl.when(c == 0)
    def _():
        g0_own.start()
        for cp in hub_copies():
            cp.start()

    def s_arrive():
        @pl.when(r == 0)
        def _():
            own_s.wait()

        @pl.when(r != 0)
        def _():
            arrive("es", ea.at[x, z, core, :, pl.ds(0, NB)])

    def corner_relay():
        @pl.when(r == 0)
        def _():
            @pl.when(c == 0)
            def _():
                cp = local("corner_own", gb.at[pl.ds(0, 16)], piece)
                cp.start()
                cp.wait()

            @pl.when(c != 0)
            def _():
                corner_piece(0).wait_recv()

            for cp in row0_copies("g"):
                cp.start()
            own_g.start()

    def corner_arrive():
        @pl.when(r == 0)
        def _():
            own_g.wait()
            own_r.wait()

        @pl.when(r != 0)
        def _():
            arrive("eg", ea.at[x, z, core, :, pl.ds(NB, 256)])
            arrive("er", rr)

    def block(xx, zz):
        return sg.at[xx, zz]

    def block_lo(xx, zz):
        return sg.at[xx, zz, pl.ds(0, 16)]

    def block_hi(xx, zz):
        return sg.at[xx, zz, pl.ds(16, 16)]

    def span_z(s):
        full = s < 4
        arrive("zp%d" % (s - 1), (block if full else block_lo)(x, zs[-s]))
        arrive("zm%d" % (s - 1), (block if full else block_hi)(x, zs[s]))
        if s < 4:
            p, m = (block, block) if s < 3 else (block_lo, block_hi)
            send("zp%d" % s, p(x, zs[-s]), p(x, zs[-s]), (r, zp))
            send("zm%d" % s, m(x, zs[s]), m(x, zs[s]), (r, zm))

    def span_x(k):
        b = block(x, zs[ORDER[k]])
        send("xp%d" % k, b, b, (r, xp))
        send("xm%d" % k, b, b, (r, xm))

    def span_relay(k):
        zz = zs[ORDER[k]]
        arrive("xp%d" % k, block(xs[-1], zz))
        send("xxp%d" % k, block_lo(xs[-1], zz), block_lo(xs[-1], zz), (r, xp))
        arrive("xm%d" % k, block(xs[1], zz))
        send("xxm%d" % k, block_hi(xs[1], zz), block_hi(xs[1], zz), (r, xm))

    def span_end(k):
        zz = zs[ORDER[k]]
        arrive("xxp%d" % k, block_lo(xs[2], zz))
        arrive("xxm%d" % k, block_hi(xs[2], zz))

    x2 = (x + 2) % NX * NZ + z

    lanes_of = {"s": pl.ds(0, NB), "g": pl.ds(NB, 256)}

    def e_z_send(kind):
        b = ea.at[x, z, core, :, lanes_of[kind]]
        for d in range(1, NZ):
            send("ez%s%d" % (kind, d), b, b, (r, x * NZ + (z + d) % NZ))

    def e_z_arrive(kind):
        for d in range(1, NZ):
            arrive("ez%s%d" % (kind, d), ea.at[x, (z + NZ - d) % NZ, core, :, lanes_of[kind]])

    def e_core(kind, d):
        b = ea.at[xs[d], :, core, :, lanes_of[kind]]
        send("ec%s%d" % (kind, d), b, b, (other, c))

    def e_x_send(kind):
        b = ea.at[x, :, core, :, lanes_of[kind]]
        send("exp" + kind, b, b, (r, xp))
        send("exm" + kind, b, b, (r, xm))
        send("ex2" + kind, b, b, (r, x2))
        e_core(kind, 0)

    def e_x_arrive(kind):
        for tag, d in (("exp", -1), ("exm", 1), ("ex2", 2)):
            arrive(tag + kind, ea.at[xs[d], :, core, :, lanes_of[kind]])
            e_core(kind, d)

    def e_core_arrive():
        for kind in "sg":
            for d in (0, -1, 1, 2):
                arrive("ec%s%d" % (kind, d), ea.at[xs[d], :, 1 - core, :, lanes_of[kind]])

    def g_arrive():
        if phase[0] != "go":
            return

        direct = jnp.logical_and(jnp.logical_and(c != 0, c != NZ), c != 3 * NZ)

        @pl.when(direct)
        def _():
            arrive("piece", g0.at[x, z])

        @pl.when(jnp.logical_or(c == NZ, c == 3 * NZ))
        def _():
            local("g0_hub", q.at[pl.ds(0, 64)], g0.at[x, z]).wait()

        @pl.when(c == 0)
        def _():
            g0_own.wait()

    def g_x_send():
        b = g0.at[x, z]
        send("gxp", b, b, (r, xp))
        send("gxm", b, b, (r, xm))
        send("gx2", b, b, (r, x2))
        for d in (1, 2, 3):
            send("yg%d" % d, b, yg.at[d - 1], ((r + 2 * d) % NROW, c))

    def g_x_arrive(j):
        arrive(("gxp", "gxm", "gx2")[j - 1], g0.at[xs[(0, -1, 1, 2)[j]], z])

    def g_z(j, s):
        xx = xs[(0, -1, 1, 2)[j]]
        for sign, tag, peer in ((-1, "p", zp), (1, "m", zm)):
            b = g0.at[xx, zs[sign * s]]
            if s >= 3:
                half = g0.at[xx, zs[sign * s], pl.ds(0 if tag == "p" else 32, 32)]
            if s:
                arrive("gz%s%d%d" % (tag, j, s - 1), half if s == 4 else b)
            if s < 4:
                h = half if s == 3 else b
                send("gz%s%d%d" % (tag, j, s), h, h, (r, peer))

    def route(name, src, dst, target):
        if phase[0] != "near":
            @pl.when(target != c)
            def _():
                far = remote(name, name.rstrip("0123456789"), src, dst, (r, target))
                if phase[0] == "go":
                    far.start()
                else:
                    far.wait_send()

        if phase[0] != "drain":
            @pl.when(target == c)
            def _():
                near = local(name, src, dst)
                if phase[0] == "go":
                    near.start()
                else:
                    near.wait()

    is_source = r == z
    relays = jnp.logical_and(receiver, jnp.logical_not(is_source))
    tile = pl.ds(pl.multiple_of(x * NB, NB), NB)

    def share(k):
        zz = zs[ORDER[k]]
        src, dst = sg.at[:, zz, :, tile], sc.at[:, zz]

        @pl.when(is_source)
        def _():
            for tag, dev in (("c", other), ("2", (r + 2) % NROW), ("6", (r + 6) % NROW), ("4", (r + 4) % NROW)):
                cp = remote("sh%d_%s" % (k, tag), "sh%d" % k, src, dst, (dev, c))
                if phase[0] == "go":
                    cp.start()
                else:
                    cp.wait_send()
            if phase[0] == "go":
                local("sh%d" % k, src, dst).start()

    def share_next(k):
        zz = zs[ORDER[k]]
        src, dst = sg.at[:, zz, :, tile], sc.at[:, zz]
        if phase[0] == "go":
            @pl.when(is_source)
            def _():
                local("sh%d" % k, src, dst).wait()

            @pl.when(jnp.logical_not(is_source))
            def _():
                arrive("sh%d" % k, dst)

        @pl.when(relays)
        def _():
            cp = remote("sh%d_c" % k, "sh%d" % k, dst, dst, (other, c))
            if phase[0] == "go":
                cp.start()
            else:
                cp.wait_send()

    def gc_routes():
        for d in range(4):
            row = (r + NROW - 2 * d) % NROW
            if d:
                arrive("yg%d" % d, yg.at[d - 1])
            route("gc%d" % d, yg.at[d - 1] if d else g0.at[x, z], gc.at[z], x * NZ + row)

    def forward(name, ref, part, piece_name, routes):
        if phase[0] == "go":
            phase[0] = "near"
            routes()
            phase[0] = "go"

        @pl.when(receiver)
        def _():
            arrive(piece_name, part)
            send(name, ref, ref, (other, c))

    def gc_forward():
        forward("gcf", gc, gc.at[pl.ds(0, NZ - 1)], "gc", gc_routes)

    def shared_arrive():
        @pl.when(jnp.logical_not(receiver))
        def _():
            arrive("gcf", gc)

    span_z(1)
    span_x(1)
    span_x(2)
    s_arrive()
    e_z_send("s")
    hub_pass(0)
    corner_relay()
    span_z(2)
    hub_pass(1)
    span_relay(0)
    corner_arrive()
    e_z_send("g")
    e_z_arrive("s")
    e_x_send("s")
    e_z_arrive("g")
    e_x_send("g")
    span_z(3)
    span_x(3)
    span_x(4)
    span_relay(1)
    g_arrive()
    g_x_send()
    g_z(0, 0)
    e_x_arrive("s")
    e_x_arrive("g")
    span_z(4)
    span_x(5)
    span_x(6)
    span_relay(2)
    for j in (1, 2, 3):
        g_x_arrive(j)
        g_z(j, 0)
    g_z(0, 1)
    span_x(7)
    own.wait()
    e_core_arrive()

    s0 = ea[:, :, :, :, :NB].reshape(TOKENS, NB)
    g00 = jnp.concatenate(
        [ea[:, :, h, :, NB:].reshape(NB, 256) for h in range(2)], axis=1).astype(F32)
    ridge0 = jnp.concatenate([rr[i:i + 1] for i in range(4)], axis=1)
    corner = g00 + lax.dot_general(s0, s0, TN, preferred_element_type=F32) * (1.0 / TOKENS) + eye(NB) * ridge0
    above = lax.broadcasted_iota(jnp.int32, (NB, NB), 0) < lax.broadcasted_iota(jnp.int32, (NB, NB), 1)
    w[:, :NB] = jnp.where(above, corner.T, corner)
    w[:, NB:] = eye(NB)

    slots = [
        lambda: (span_relay(3), span_end(0), share(0)),
        lambda: (g_z(1, 1), g_z(2, 1), g_z(3, 1)),
        lambda: (span_end(1), share(1)),
        lambda: (span_relay(4), gc_routes()),
        lambda: (g_z(0, 2), g_z(1, 2), share_next(0)),
        lambda: (g_z(2, 2), g_z(3, 2)),
        lambda: (span_end(2), share(2), span_relay(5), share_next(1)),
        lambda: (g_z(0, 3), g_z(1, 3)),
        lambda: (span_end(3), share(3), g_z(2, 3), g_z(3, 3)),
        lambda: (span_relay(6), share_next(2)),
        lambda: (span_end(4), share(4), share_next(3)),
        lambda: (span_relay(7), gc_forward()),
        lambda: (span_end(5), share(5), share_next(4)),
        lambda: [g_z(j, 4) for j in range(4)],
        lambda: (span_end(6), share(6), share_next(5)),
        lambda: (span_end(7), share(7), share_next(6)),
    ]
    for kb in range(NB // 128):
        lo, hi = kb * 128, kb * 128 + 128
        m = factor_block(w[lo:hi, lo:hi], lambda i: slots[4 * kb + i]())
        head = jnp.dot(m, w[lo:hi, lo:NB + hi], precision=HI, preferred_element_type=F32)
        w[lo:hi, lo:NB + hi] = head
        if hi < NB:
            w[hi:NB, hi:NB + hi] -= lax.dot_general(
                head[:, 128:NB - lo], head[:, 128:], TN, precision=HI, preferred_element_type=F32)

    @pl.when(c != 0)
    def _():
        lead_in.wait()
        gram_in.wait()

    def products(h):
        group = [zs[ORDER[i]] for i in range(4 * h, 4 * h + 4)]
        right = jnp.concatenate([
            jnp.concatenate([sc[:, zz].reshape(128, NB), ea[:, zz, :, :, :NB].reshape(128, NB)], axis=1)
            for zz in group], axis=0)

        @pl.loop(0, NROW // 2)
        def _(k):
            part = pl.ds(pl.multiple_of(k * NB, NB), NB)
            a = jnp.concatenate([sg[:, zz, :, part].reshape(128, NB) for zz in group], axis=0)
            prod = lax.dot_general(a, right, TN, preferred_element_type=F32) * (1.0 / TOKENS)
            if h:
                acc[part, :] += prod[:, :NB]
                a0[part, :] = (p0[part, :] + prod[:, NB:] + g0[k].reshape(NB, NB).astype(F32)).astype(BF16)
            else:
                acc[part, :] = prod[:, :NB] + gv[part, :]
                p0[part, :] = prod[:, NB:]

                @pl.when(jnp.logical_and(r == z, k == x))
                def _():
                    four = ridge[pl.ds(4 * k, 4), :]
                    acc[part, :] += eye(NB) * jnp.concatenate([four[i:i + 1] for i in range(4)], axis=1)

    products(0)
    shared_arrive()
    share_next(7)

    @pl.when(c != 0)
    def _():
        ac0 = gc[...].reshape(NB, NB).astype(F32) + lax.dot_general(
            sc[...].reshape(TOKENS, NB), ea[:, :, :, :, :NB].reshape(TOKENS, NB), TN, preferred_element_type=F32) * (1.0 / TOKENS)
        high, low = split(w[:, NB:])
        b = ac0.astype(BF16)
        nt = (((1,), (1,)), ((), ()))
        y = (lax.dot_general(high, b, nt, preferred_element_type=F32)
             + lax.dot_general(low, b, nt, preferred_element_type=F32)).astype(BF16)
        zv[...] = (lax.dot_general(high, y, TN, preferred_element_type=F32)
                   + lax.dot_general(low, y, TN, preferred_element_type=F32)).astype(BF16)

    @pl.when(c == 0)
    def _():
        zv[...] = (-w[:, NB:].T).astype(BF16)

    z_copy = local("z_out", zv, z_out)
    z_copy.start()
    products(1)

    @pl.when(r == 0)
    def _():
        a0[:NB, :] = jnp.zeros((NB, NB), BF16)

    @pl.when(c == 0)
    def _():
        acc[...] = jnp.zeros(acc.shape, F32)

        @pl.when(r == 0)
        def _():
            acc[:NB, :] = jnp.where(above, 0.0, w[:, :NB].T)

    a_copies = [local("a0_out", a0, a0_out), local("acc_out", acc, acc_out)]
    for cp in a_copies:
        cp.start()

    phase[0] = "drain"
    own_sends()
    hub_pass(0)
    hub_pass(1)
    for kind in "sg":
        e_z_send(kind)
        e_x_send(kind)
        e_x_arrive(kind)
    g_x_send()
    for s in range(5):
        for j in range(4):
            g_z(j, s)
    for s in range(1, 5):
        span_z(s)
    for k in range(8):
        if k:
            span_x(k)
        span_relay(k)
    for k in range(8):
        share(k)
        share_next(k)
    gc_routes()
    gc_forward()

    @pl.when(r == 0)
    def _():
        for cp in row0_copies("s") + row0_copies("g"):
            cp.wait_send()

    @pl.when(c == 0)
    def _():
        for cp in hub_copies():
            cp.wait_send()

        @pl.when(r == 0)
        def _():
            @pl.loop(1, NCOL)
            def _(t):
                corner_piece(t).wait_send()

    for cp in [z_copy] + a_copies:
        cp.wait()


def panel(span, gram, ridge):
    rows, cols = gram.shape
    dma = pltpu.SemaphoreType.DMA
    scratch = [
        ((NX, NZ, 32, rows), BF16), ((NX, NZ, 64, NB), BF16), ((NX, NZ, 2, 16, 768), BF16),
        ((NX, NZ, 32, NB), BF16), ((NZ, 64, NB), BF16), ((3, 64, NB), BF16),
        ((8, 128), F32), ((16, NB), BF16), ((rows, cols), F32), ((rows, cols), BF16),
        ((NB, 2 * NB), F32), ((rows, cols), F32), ((rows, cols), F32), ((rows, cols), BF16),
        ((NB, NB), BF16)]
    return pl.pallas_call(
        panel_kernel,
        out_shape=[jax.ShapeDtypeStruct((rows, cols), F32), jax.ShapeDtypeStruct((rows, cols), BF16),
                   jax.ShapeDtypeStruct((NB, NB), BF16)],
        in_specs=[pl.BlockSpec(memory_space=pl.ANY)] * 2 + [pl.BlockSpec(memory_space=pltpu.VMEM)],
        out_specs=[pl.BlockSpec(memory_space=pl.ANY)] * 3,
        scratch_shapes=[pltpu.VMEM(*s) for s in scratch] + [
            pltpu.VMEM((NB, NB), BF16), dma((240,)), dma((240,)), dma((40,)), dma((NCOL,)), dma((1,))],
        compiler_params=pltpu.CompilerParams(
            collective_id=0, has_side_effects=True, vmem_limit_bytes=56 * 2**20),
    )(span, gram, ridge.reshape(16, 128))


def finish_kernel(acc, a0, zc, out):
    out[...] = acc[...] - jnp.dot(a0[...], zc[...], preferred_element_type=F32)


def finish(acc, a0, zc):
    rows, cols = acc.shape
    step = 1024
    return pl.pallas_call(
        finish_kernel,
        grid=(rows // step,),
        out_shape=jax.ShapeDtypeStruct((rows, cols), F32),
        in_specs=[pl.BlockSpec((step, cols), lambda i: (i, 0)), pl.BlockSpec((step, NB), lambda i: (i, 0)),
                  pl.BlockSpec((NB, cols), lambda i: (0, 0))],
        out_specs=pl.BlockSpec((step, cols), lambda i: (i, 0)),
    )(acc, a0, zc)


def on_device(span, gram, ridge):
    return finish(*panel(span, gram, ridge))


def solution(mesh):
    placed = (P("col", "row"), P("row", "col"), P("row"))
    return jax.shard_map(
        on_device, mesh=mesh, in_specs=placed, out_specs=P("row", "col"), check_vma=False
    )
```
